128 devices in a mesh: site: 8 (over y, x_hi), op: 16 (over x_lo, z, core).
Axes of the slice: x: 4 (x_hi: 2, x_lo: 2; x = x_hi * 2 + x_lo), y: 4, z: 4, core: 2. Of those that a mesh axis runs over, the one named last changes fastest.
Arguments:
- mps: bfloat16 [8, 4, 4, 16, 128, 128], P('site'), may hold values from -0.4375 to 0.4375
- sector_map: int32 [8, 4, 16], P('site'), may hold values from 0 to 15, each once within a row
- live_rows: int32 [8, 16], P('site'), may hold values from 32 to 128, as said below
- term_mask: int32 [8, 32, 4], P('site', 'op'), may hold values 0 or 1
- term_coef: float32 [8, 32, 4], P('site', 'op'), may hold values from 0.8 to 2
- block_coef: float32 [8, 32], P('site', 'op'), may hold values from -1.2 to 1.2
- env_terms: bfloat16 [4, 32, 16, 128, 128], P(None, 'op'), may hold values from -6 to 6
- env_block: bfloat16 [4, 16, 128, 128], P(None, None, 'op'), may hold values from -6 to 6
Outputs:
- out_terms: bfloat16 [8, 4, 32, 16, 128, 128], P('site', None, 'op')
- out_block: bfloat16 [8, 4, 16, 128, 128], P('site', None, None, 'op')
The draws below stay inside these ranges and needn't reach their ends.
Inputs may be any that keep to these rules, and one draw needn't show every extreme that they name: `sector_map`: each row along the last dimension is a permutation of the 16 sectors. `live_rows`: every site has a sector with all 128 states live.
All inputs are finite; a program needn't handle non-finite values. No bound on the sum of `term_mask` on one device may be relied on, other than what follows from the above.
Results may differ from the reference program's by a relative error of at most 0.034.
Values may be sent and summed in bfloat16 or wider, within the bound.
A program may use at most 192 MiB of HBM per device.

```python
import math
import jax
import jax.numpy as jnp

B = 128
NSEC = 16
NPHYS = 4
ROOTS = 4
TERMS = 32
SITES = 8


def draw_live_rows(key, part):
    key = jax.random.fold_in(key, 11)
    first_key, second_key = jax.random.split(key)
    counts = jax.random.randint(first_key, (SITES, NSEC), B // 4, B + 1)
    chosen = jax.random.randint(second_key, (SITES, 1), 0, NSEC)
    return jnp.where(jnp.arange(NSEC)[None, :] == chosen, B, counts).astype(jnp.int32)


def plant(drawn, key, least, top_value):
    dims = drawn.shape
    place = [jax.random.randint(jax.random.fold_in(key, axis), (), 0, dims[axis]) for axis in range(len(dims))]
    drawn = drawn.at[tuple(place)].set(least)
    longest = dims.index(max(dims))
    place[longest] = (place[longest] + 1) % dims[longest]
    return drawn.at[tuple(place)].set(top_value)


def shard_levels(rng, dims, cuts, smallest, largest):
    def one(axis_at, blocks):
        draws = jax.random.uniform(jax.random.fold_in(jax.random.fold_in(rng, 6), axis_at), (blocks,), jnp.float32, smallest / len(cuts), largest / len(cuts))
        return jnp.repeat(jnp.exp(draws), dims[axis_at] // blocks).reshape((-1,) + (1,) * (len(dims) - axis_at - 1))

    loudness = one(*cuts[0])
    for cut in cuts[1:]:
        loudness = loudness * one(*cut)
    return loudness


def scatter_about(key, dims, width, most, pieces=(), kind=jnp.bfloat16):
    level = shard_levels(key, dims, pieces, -0.22, 0.18) if pieces else 1.0
    values = jax.random.normal(key, dims, jnp.float32) * width * level
    return jnp.minimum(jnp.maximum(values, -most), most).astype(kind)


def setup_inputs(seed: int = 0) -> dict:
    keys = jax.random.split(jax.random.key(seed), 9)
    return {
        "mps": scatter_about(keys[0], (SITES, ROOTS, NPHYS, NSEC, B, B), (3 * B // 2) ** -0.5, 0.4375, ((0, 8),)),
        "sector_map": jax.vmap(lambda own: jax.random.permutation(own, NSEC))(jax.random.split(keys[1], SITES * NPHYS)).reshape((SITES, NPHYS, NSEC)).astype(jnp.int32),
        "live_rows": draw_live_rows(jax.random.fold_in(keys[8], 71), 0),
        "term_mask": plant((jax.random.randint(keys[3], (SITES, TERMS, NPHYS), 0, 4) < 3).astype(jnp.int32), jax.random.fold_in(keys[3], 1), 0, 1),
        "term_coef": jnp.clip(jnp.exp(math.log(2.0) - 0.9162907 * jax.random.uniform(keys[4], (SITES, TERMS, NPHYS), jnp.float32) ** shard_levels(keys[4], (SITES, TERMS, NPHYS), ((0, 8), (1, 16)), -0.2, 0.2)), 0.8, 2.0),
        "block_coef": scatter_about(keys[5], (SITES, TERMS), 0.2, 1.2, ((0, 8), (1, 16)), jnp.float32),
        "env_terms": scatter_about(keys[6], (ROOTS, TERMS, NSEC, B, B), 1.0, 6.0, ((1, 16),)),
        "env_block": scatter_about(keys[7], (ROOTS, NSEC, B, B), 1.0, 6.0, ((2, 16),)),
    }


def reference(mps, sector_map, live_rows, term_mask, term_coef, block_coef, env_terms, env_block):
    columns = jnp.arange(B)
    all_terms = []
    all_blocks = []
    for root in range(ROOTS):
        terms = env_terms[root]
        block = env_block[root]
        root_terms = []
        root_blocks = []
        for site_idx in range(SITES):
            keep = columns[None, None, :] < live_rows[site_idx][:, None, None]
            amat = jnp.where(keep, mps[site_idx, root], jnp.zeros_like(mps[site_idx, root]))
            afloat = amat.astype(jnp.float32)
            weights = term_coef[site_idx] * term_mask[site_idx].astype(jnp.float32)
            source = jnp.take(terms, sector_map[site_idx], axis=1).astype(jnp.float32)
            product = jnp.einsum('ksrab,srbc->ksrac', source, afloat)
            scaled = (product * weights[:, :, None, None, None]).astype(jnp.bfloat16)
            mixed = jnp.einsum('srab,ksrac->krbc', afloat, scaled.astype(jnp.float32))
            feed = jnp.take(block, sector_map[site_idx], axis=0).astype(jnp.float32)
            moved = jnp.einsum('srab,srbc->srac', feed, afloat).astype(jnp.bfloat16)
            own = jnp.einsum('srab,srac->rbc', afloat, moved.astype(jnp.float32))
            pairs = jnp.einsum('k,krbc->rbc', block_coef[site_idx], mixed)
            block = (own + pairs).astype(jnp.bfloat16)
            terms = mixed.astype(jnp.bfloat16)
            root_terms.append(terms)
            root_blocks.append(block)
        all_terms.append(jnp.stack(root_terms, 0))
        all_blocks.append(jnp.stack(root_blocks, 0))
    out_terms = jnp.stack(all_terms, 1)
    out_block = jnp.stack(all_blocks, 1)
    return out_terms, out_block
```

```python
import functools

import jax
import jax.numpy as jnp
from jax import lax
from jax.experimental import pallas as pl
from jax.experimental.pallas import tpu as pltpu
from jax.sharding import PartitionSpec as P

MESH = pl.DeviceIdType.MESH
F32 = jnp.float32
BF16 = jnp.bfloat16
SITES, ROOTS, STATES, SECTORS, B = 8, 4, 4, 16, 128
CHAINS = 3
UNROLL = 4


class Place:
    def __init__(self):
        site = lax.axis_index("site")
        op = lax.axis_index("op")
        self.site, self.op = site, op
        self.h, self.y = lax.rem(site, 2), site // 2
        self.l, self.z, self.c = op // 8, lax.rem(op // 2, 4), lax.rem(op, 2)
        self.x = 2 * self.h + self.l

    def along_x(self, by):
        x = lax.rem(self.x + by, 4)
        return {"site": 2 * self.y + x // 2, "op": 8 * lax.rem(x, 2) + 2 * self.z + self.c}

    def along_z(self, by):
        z = lax.rem(self.z + by, 4)
        return {"site": self.site, "op": 8 * self.l + 2 * z + self.c}

    def along_y(self, by):
        return {"site": 2 * lax.rem(self.y + by, 4) + self.h, "op": self.op}

    def row(self, y):
        return {"site": 2 * y + self.h, "op": self.op}

    def sibling(self):
        return {"site": self.site, "op": self.op + 1 - 2 * self.c}

    def along_site(self, by):
        return {"site": lax.rem(self.site + by, SITES), "op": self.op}

    def group(self, g):
        return {"site": self.site, "op": 2 * g + self.c}


def kernel(ints_ref, floats_ref, rows_ref, mps_ref, env_ref, out_terms, out_block, *scratch):
    scratch = list(scratch)
    a_bufs = [scratch.pop(0) for _ in range(SITES)]
    x_bufs = [scratch.pop(0) for _ in range(SITES + 1)]
    h_bufs = [scratch.pop(0) for _ in range(SITES)]
    (s_buf, core_buf, part_buf, ring_buf, final_buf, ints_all, floats_all, ints, floats,
     param_s, param_r, param_l, y_s, y_r, xa_s, xa_r, za_s, za_r, xb_s, xb_r, zb_s, zb_r, c_s, c_r,
     env_l, out_s, out_r, h1_s, h1_r, h2_s, h2_r, h3_s, h3_r) = scratch
    me = Place()

    def remote(src, dst, send, recv, device):
        return pltpu.make_async_remote_copy(
            src_ref=src, dst_ref=dst, send_sem=send, recv_sem=recv, device_id=device, device_id_type=MESH
        )

    def arrival(dst, recv):
        pltpu.make_async_copy(dst, dst, recv).wait()

    barrier = pltpu.get_barrier_semaphore()
    partners = [me.along_site(d) for d in range(1, SITES)]
    partners += [me.along_x(1), me.along_x(3)]
    partners += [me.along_z(d) for d in (1, 2, 3)]
    partners += [me.sibling()]
    g_me = me.op // 2
    partners += [
        {"site": me.site, "op": 8 * (1 - me.l) + 2 * lax.rem(me.z + d, 4) + me.c} for d in (1, 2, 3)
    ]
    for device in partners:
        pl.semaphore_signal(barrier, inc=1, device_id=device, device_id_type=MESH)
    pl.semaphore_wait(barrier, len(partners))

    sends = []

    def start(copy):
        copy.start()
        sends.append(copy)

    for d in range(1, SITES):
        start(remote(ints_ref, ints_all.at[me.site], param_s.at[0, d], param_r.at[0, me.site], me.along_site(d)))
        start(remote(floats_ref, floats_all.at[me.site], param_s.at[1, d], param_r.at[1, me.site], me.along_site(d)))

    def piece(q):
        return mps_ref.at[q, :, me.op]

    def slot(i):
        return a_bufs[i].at[me.l, me.z, me.c]

    def own(i):
        return me.h == i % 2

    for i in range(SITES):
        @pl.when(me.site == i)
        def _():
            for d in (1, 2, 3):
                q = lax.rem(me.y + d, 4)
                remote(piece(q), slot(i), y_s.at[d], y_r.at[i // 2], me.along_y(d)).start()
            pltpu.make_async_copy(piece(me.y), slot(i), y_r.at[i // 2]).start()

    env_copies = []
    for k in range(2):
        copy = pltpu.make_async_copy(env_ref.at[me.y, k], x_bufs[0].at[:, k], env_l.at[k])
        copy.start()
        env_copies.append(copy)

    row_group = lax.broadcasted_iota(jnp.int32, (B, B), 0) // 8
    def init(e, _):
        tiled = jnp.concatenate([rows_ref[e]] * (B // 8), axis=0)
        x_bufs[0][e, 2] = jnp.where(row_group == me.op, tiled, 0.0).astype(BF16)
        return 0
    lax.fori_loop(0, SECTORS, init, 0)

    first, second = pl.ds(0, 2), pl.ds(2, 2)

    def p1(i):
        @pl.when(own(i))
        def _():
            arrival(slot(i), y_r.at[i // 2])
            a = a_bufs[i]
            for d in (1, 3, 2):
                part = a.at[me.l, me.z, me.c, first]
                remote(part, part, xa_s.at[i, d - 1], xa_r.at[i, me.l], me.along_x(d)).start()
                part = a.at[me.l, me.z, me.c, second]
                remote(part, part, za_s.at[i, d - 1], za_r.at[i, me.z], me.along_z(d)).start()

    def p2(i):
        a = a_bufs[i]
        for l in range(2):
            @pl.when(jnp.logical_not(jnp.logical_and(own(i), me.l == l)))
            def _():
                arrival(a.at[l, me.z, me.c, first], xa_r.at[i, l])
        for d in (1, 3, 2):
            part = a.at[:, me.z, me.c, first]
            start(remote(part, part, zb_s.at[i, d - 1], zb_r.at[i, me.z], me.along_z(d)))

        @pl.when(own(i))
        def _():
            for d in (1, 3, 2):
                z = lax.rem(me.z + d, 4)
                arrival(a.at[me.l, z, me.c, second], za_r.at[i, z])
            for d in (1, 3, 2):
                part = a.at[me.l, :, me.c, second]
                remote(part, part, xb_s.at[i, d - 1], xb_r.at[i, me.l], me.along_x(d)).start()

    def p3(i):
        a = a_bufs[i]
        for d in (1, 3, 2):
            z = lax.rem(me.z + d, 4)
            arrival(a.at[:, z, me.c, first], zb_r.at[i, z])
        for l in range(2):
            @pl.when(jnp.logical_not(jnp.logical_and(own(i), me.l == l)))
            def _():
                arrival(a.at[l, :, me.c, second], xb_r.at[i, l])
        part = a.at[:, :, me.c]
        start(remote(part, part, c_s.at[i], c_r.at[i], me.sibling()))

    def p4(i):
        arrival(a_bufs[i].at[:, :, 1 - me.c], c_r.at[i])

    column = lax.broadcasted_iota(jnp.int32, (1, B), 1)
    row = lax.broadcasted_iota(jnp.int32, (B, 1), 0)

    def multiply(i):
        a, x, new, h = a_bufs[i], x_bufs[i], x_bufs[i + 1], h_bufs[i]

        def first_product(e, _):
            wide, scale = [], []
            for s in range(STATES):
                r = ints[i, 0, 64 + s * SECTORS + e]
                wide.append(a[r // 8, lax.rem(r // 2, 4), lax.rem(r, 2), s])
                live = column < ints[i, 1, r]
                scale.append(
                    [jnp.where(live, floats[i, 0, k * STATES + s], 0.0) for k in range(2)]
                    + [jnp.where(live, 1.0, 0.0)]
                )
            product = jnp.dot(
                x[e].reshape(CHAINS * B, B), jnp.concatenate(wide, axis=1), preferred_element_type=F32
            )
            for s in range(STATES):
                s_buf[e, s] = jnp.concatenate(
                    [
                        (product[k * B : (k + 1) * B, s * B : (s + 1) * B] * scale[s][k]).astype(BF16)
                        for k in range(CHAINS)
                    ],
                    axis=1,
                )
            return 0

        lax.fori_loop(0, SECTORS, first_product, 0, unroll=UNROLL)

        def second_product(pair, _):
            blocks = []
            for part in range(2):
                r = 2 * pair + part
                scaled = jnp.concatenate([s_buf[ints[i, 0, s * SECTORS + r], s] for s in range(STATES)], axis=0)
                tensor = a[pair // 4, lax.rem(pair, 4), part].reshape(STATES * B, B)
                mixed = lax.dot_general(
                    tensor, scaled, (((0,), (0,)), ((), ())), preferred_element_type=F32
                )
                mixed = jnp.where(row < ints[i, 1, r], mixed, 0.0)
                chains = [mixed[:, k * B : (k + 1) * B] for k in range(CHAINS)]
                chains[2] = chains[2] + floats[i, 0, 8] * chains[0] + floats[i, 0, 9] * chains[1]
                for k in range(CHAINS):
                    new[r, k] = chains[k].astype(BF16)
                blocks.append(chains[2].reshape(SECTORS, 8, B))
            h[:, :, pair] = jnp.concatenate(blocks, axis=1).astype(BF16).reshape(8, 2, 16, B)
            return 0

        lax.fori_loop(0, SECTORS // 2, second_product, 0, unroll=UNROLL // 2)

    def out(i):
        target = i // 2

        @pl.when(own(i))
        def _():
            for k in range(2):
                src, dst = x_bufs[i + 1].at[:, k], out_terms.at[me.y, k]

                @pl.when(me.y == target)
                def _():
                    pltpu.make_async_copy(src, dst, out_r.at[me.y, k]).start()

                @pl.when(me.y != target)
                def _():
                    remote(src, dst, out_s.at[target, k], out_r.at[me.y, k], me.row(target)).start()

    def h1(i):
        @pl.when(own(i))
        def _():
            remote(h_bufs[i].at[:, 1 - me.c], core_buf.at[i // 2], h1_s.at[i // 2], h1_r.at[i // 2], me.sibling()).start()

    def h2(i):
        n = i // 2

        @pl.when(own(i))
        def _():
            arrival(core_buf.at[n], h1_r.at[n])
            for g in range(8):
                part_buf[n, g] = (
                    h_bufs[i][g, me.c].astype(F32) + core_buf[n, g].astype(F32)
                ).astype(BF16)
            for g in range(8):
                @pl.when(g_me != g)
                def _():
                    remote(part_buf.at[n, g], ring_buf.at[n, g_me], h2_s.at[n, g], h2_r.at[n, g_me], me.group(g)).start()

    def h3(i):
        n = i // 2

        @pl.when(own(i))
        def _():
            total = part_buf[n, g_me].astype(F32)
            for d in range(1, 8):
                g = lax.rem(g_me + d, 8)
                arrival(ring_buf.at[n, g], h2_r.at[n, g])
                total = total + ring_buf[n, g].astype(F32)
            final_buf[n] = total.astype(BF16)

            @pl.when(me.y == n)
            def _():
                pltpu.make_async_copy(final_buf.at[n], out_block.at[me.y], h3_r.at[me.y]).start()

            @pl.when(me.y != n)
            def _():
                remote(final_buf.at[n], out_block.at[me.y], h3_s.at[n], h3_r.at[me.y], me.row(n)).start()

    p1(0)
    ints_all[me.site] = ints_ref[...]
    floats_all[me.site] = floats_ref[...]
    for d in range(1, SITES):
        site = lax.rem(me.site + d, SITES)
        arrival(ints_all.at[site], param_r.at[0, site])
        arrival(floats_all.at[site], param_r.at[1, site])
    to_smem = [
        pltpu.make_async_copy(ints_all, ints, param_l.at[0]),
        pltpu.make_async_copy(floats_all, floats, param_l.at[1]),
    ]
    for copy in to_smem:
        copy.start()
    p1(1)
    p2(0)
    for copy in to_smem + env_copies:
        copy.wait()
    p1(2)
    p2(1)
    p3(0)
    for i in range(SITES + 2):
        if i + 3 < SITES:
            p1(i + 3)
        if i + 2 < SITES:
            p2(i + 2)
        if i + 1 < SITES:
            p3(i + 1)
        if 0 <= i - 1 < SITES:
            h2(i - 1)
        if 0 <= i - 2 < SITES:
            h3(i - 2)
        if i < SITES:
            p4(i)
            multiply(i)
            out(i)
            h1(i)

    for q in range(ROOTS):
        for k in range(2):
            arrival(out_terms.at[q, k], out_r.at[q, k])
        arrival(out_block.at[q], h3_r.at[q])
    for copy in sends:
        copy.wait_send()

    def left(src, sem):
        pltpu.make_async_copy(src, src, sem).wait()

    for d in (1, 2, 3):
        left(piece(0), y_s.at[d])
    for i in range(SITES):
        @pl.when(own(i))
        def _():
            for d in (1, 2, 3):
                left(a_bufs[i].at[0, 0, 0, first], xa_s.at[i, d - 1])
                left(a_bufs[i].at[0, 0, 0, first], za_s.at[i, d - 1])
                left(a_bufs[i].at[0, :, 0, first], xb_s.at[i, d - 1])
            left(core_buf.at[i // 2], h1_s.at[i // 2])
            for g in range(8):
                @pl.when(g_me != g)
                def _():
                    left(part_buf.at[i // 2, g], h2_s.at[i // 2, g])

            @pl.when(me.y != i // 2)
            def _():
                for k in range(2):
                    left(x_bufs[i + 1].at[:, k], out_s.at[i // 2, k])
                left(final_buf.at[i // 2], h3_s.at[i // 2])


def shards(mps, sector_map, live_rows, term_mask, term_coef, block_coef, env_terms, env_block):
    row = lax.axis_index("site") // 2
    source = sector_map[0]
    inverse = jnp.sum(
        jnp.where(source[:, None, :] == jnp.arange(SECTORS)[None, :, None], jnp.arange(SECTORS)[None, None, :], 0),
        axis=2,
    ).astype(jnp.int32)
    ints = jnp.concatenate([source.reshape(-1), inverse.reshape(-1), live_rows[0], jnp.zeros((880,), jnp.int32)])
    weights = term_coef[0] * term_mask[0].astype(F32)
    floats = jnp.concatenate([weights.reshape(-1), block_coef[0], jnp.zeros((1014,), F32)])
    rows = lax.dynamic_index_in_dim(env_block, row, 0, False).astype(F32)
    dma = pltpu.SemaphoreType.DMA
    vmem = pltpu.VMEM
    scratch = [vmem((2, 4, 2, STATES, B, B), BF16)] * SITES
    scratch += [vmem((SECTORS, CHAINS, B, B), BF16)] * (SITES + 1)
    scratch += [vmem((8, 2, 8, 16, B), BF16)] * SITES
    scratch += [
        vmem((SECTORS, STATES, B, CHAINS * B), BF16),
        vmem((4, 8, 8, 16, B), BF16),
        vmem((4, 8, 8, 16, B), BF16),
        vmem((4, 8, 8, 16, B), BF16),
        vmem((4, 8, 16, B), BF16),
        vmem((SITES, 8, B), jnp.int32),
        vmem((SITES, 8, B), F32),
        pltpu.SMEM((SITES, 8, B), jnp.int32),
        pltpu.SMEM((SITES, 8, B), F32),
        dma((2, SITES)), dma((2, SITES)), dma((2,)),
        dma((4,)), dma((4,)),
        dma((SITES, 3)), dma((SITES, 2)),
        dma((SITES, 3)), dma((SITES, 4)),
        dma((SITES, 3)), dma((SITES, 2)),
        dma((SITES, 3)), dma((SITES, 4)),
        dma((SITES,)), dma((SITES,)),
        dma((2,)),
        dma((4, 2)), dma((4, 2)),
        dma((4,)), dma((4,)),
        dma((4, 8)), dma((4, 8)),
        dma((4,)), dma((4,)),
    ]
    anywhere = pl.BlockSpec(memory_space=pl.ANY)
    inside = pl.BlockSpec(memory_space=pltpu.VMEM)
    terms, block = pl.pallas_call(
        kernel,
        out_shape=(
            jax.ShapeDtypeStruct((ROOTS, 2, SECTORS, B, B), BF16),
            jax.ShapeDtypeStruct((ROOTS, 8, 16, B), BF16),
        ),
        in_specs=[inside, inside, inside, anywhere, anywhere],
        out_specs=(anywhere, anywhere),
        scratch_shapes=scratch,
        compiler_params=pltpu.CompilerParams(
            collective_id=0, has_side_effects=True, vmem_limit_bytes=56 * 2**20
        ),
        name="chains",
    )(ints.reshape(8, B), floats.reshape(8, B), rows, mps[0], env_terms)
    return terms[None], block.reshape(1, ROOTS, SECTORS, 8, B)


def solution(mesh):
    in_specs = (
        P("site", None, None, None, None, None),
        P("site", None, None),
        P("site", None),
        P("site", "op", None),
        P("site", "op", None),
        P("site", "op"),
        P(None, "op", None, None, None),
        P(None, None, "op", None),
    )
    out_specs = (P("site", None, "op", None, None, None), P("site", None, None, "op", None))
    return jax.shard_map(shards, mesh=mesh, in_specs=in_specs, out_specs=out_specs, check_vma=False)
```

```python
import functools

import jax
import jax.numpy as jnp
from jax import lax
from jax.experimental import pallas as pl
from jax.experimental.pallas import tpu as pltpu
from jax.sharding import PartitionSpec as P

MESH = pl.DeviceIdType.MESH
F32 = jnp.float32
BF16 = jnp.bfloat16
SITES, ROOTS, STATES, SECTORS, B = 8, 4, 4, 16, 128
CHAINS = 3
UNROLL = 8
EARLY = 2


class Place:
    def __init__(self):
        site = lax.axis_index("site")
        op = lax.axis_index("op")
        self.site, self.op = site, op
        self.h, self.y = lax.rem(site, 2), site // 2
        self.l, self.z, self.c = op // 8, lax.rem(op // 2, 4), lax.rem(op, 2)
        self.x = 2 * self.h + self.l

    def along_x(self, by):
        x = lax.rem(self.x + by, 4)
        return {"site": 2 * self.y + x // 2, "op": 8 * lax.rem(x, 2) + 2 * self.z + self.c}

    def along_z(self, by):
        z = lax.rem(self.z + by, 4)
        return {"site": self.site, "op": 8 * self.l + 2 * z + self.c}

    def along_y(self, by):
        return {"site": 2 * lax.rem(self.y + by, 4) + self.h, "op": self.op}

    def row(self, y):
        return {"site": 2 * y + self.h, "op": self.op}

    def sibling(self):
        return {"site": self.site, "op": self.op + 1 - 2 * self.c}

    def along_site(self, by):
        return {"site": lax.rem(self.site + by, SITES), "op": self.op}

    def group(self, g):
        return {"site": self.site, "op": 2 * g + self.c}


def kernel(map_ref, live_ref, mask_ref, coef_ref, pair_ref, block_ref, mps_ref, env_ref, out_terms, out_block, *scratch):
    scratch = list(scratch)
    a_bufs = [scratch.pop(0) for _ in range(SITES)]
    x_bufs = [scratch.pop(0) for _ in range(SITES + 1)]
    h_bufs = [scratch.pop(0) for _ in range(SITES)]
    (s_buf, core_buf, part_buf, ring_buf, final_buf, ints_all, floats_all, ints, floats,
     rows_buf, relay_buf, param_s, param_r, param_l, ya_s, ya_r, yb_s, yb_r, xa_s, xa_r, za_s, za_r, xb_s, xb_r, zb_s, zb_r, c_s, c_r,
     env_l, out_s, out_r, relay_s, relay_r, h1_s, h1_r, h2_s, h2_r, h3_s, h3_r) = scratch
    me = Place()

    def remote(src, dst, send, recv, device):
        return pltpu.make_async_remote_copy(
            src_ref=src, dst_ref=dst, send_sem=send, recv_sem=recv, device_id=device, device_id_type=MESH
        )

    def arrival(dst, recv):
        pltpu.make_async_copy(dst, dst, recv).wait()

    env_copies = [pltpu.make_async_copy(block_ref.at[me.y], rows_buf, env_l.at[2])]
    for k in range(2):
        env_copies.append(pltpu.make_async_copy(env_ref.at[me.y, k], x_bufs[0].at[:, k], env_l.at[k]))
    for copy in env_copies:
        copy.start()

    source = lax.broadcasted_iota(jnp.int32, (SECTORS, SECTORS), 0)
    target = lax.broadcasted_iota(jnp.int32, (SECTORS, SECTORS), 1)
    lane = lax.broadcasted_iota(jnp.int32, (SECTORS, B), 1)
    inverse = jnp.zeros((SECTORS, B), jnp.int32)
    for s in range(STATES):
        found = jnp.max(jnp.where(map_ref[pl.ds(s, 1), :] == source, target, 0), axis=1, keepdims=True)
        inverse = jnp.where(lane == s, found, inverse)
    ints_all[me.site] = jnp.zeros((24, B), jnp.int32)
    ints_all[me.site, pl.ds(0, STATES), pl.ds(0, SECTORS)] = map_ref[...]
    ints_all[me.site, pl.ds(4, 1), pl.ds(0, SECTORS)] = live_ref[...]
    ints_all[me.site, pl.ds(8, SECTORS), :] = inverse
    floats_all[me.site] = jnp.zeros((8, B), F32)
    floats_all[me.site, pl.ds(0, 2), pl.ds(0, STATES)] = coef_ref[...] * mask_ref[...].astype(F32)
    floats_all[me.site, pl.ds(2, 1), pl.ds(0, 2)] = pair_ref[...]

    barrier = pltpu.get_barrier_semaphore()
    partners = [me.along_site(d) for d in range(1, SITES)]
    partners += [me.along_x(1), me.along_x(3)]
    partners += [me.along_z(d) for d in (1, 2, 3)]
    partners += [me.sibling()]
    g_me = me.op // 2
    partners += [
        {"site": me.site, "op": 8 * (1 - me.l) + 2 * lax.rem(me.z + d, 4) + me.c} for d in (1, 2, 3)
    ]
    for device in partners:
        pl.semaphore_signal(barrier, inc=1, device_id=device, device_id_type=MESH)
    pl.semaphore_wait(barrier, len(partners))

    sends = []

    def start(copy):
        copy.start()
        sends.append(copy)

    for d in range(1, SITES):
        start(remote(ints_all.at[me.site], ints_all.at[me.site], param_s.at[0, d], param_r.at[0, me.site], me.along_site(d)))
        start(remote(floats_all.at[me.site], floats_all.at[me.site], param_s.at[1, d], param_r.at[1, me.site], me.along_site(d)))

    first, second = pl.ds(0, 2), pl.ds(2, 2)

    def own(i):
        return me.h == i % 2

    def first_parts(q, i):
        return [(mps_ref.at[q, first, me.l, me.z, me.c], a_bufs[i].at[me.l, me.z, me.c, first], 0)]

    def second_parts(q, i):
        if i < EARLY:
            return [(mps_ref.at[q, second, me.l, me.z, me.c], a_bufs[i].at[me.l, me.z, me.c, second], 0)]
        return [(mps_ref.at[q, 2 + n, me.l, :, me.c], a_bufs[i].at[me.l, :, me.c, 2 + n], n) for n in range(2)]

    def spread(parts, send, recv, sites):
        for i in sites:
            @pl.when(me.site == i)
            def _():
                for d in (2, 1, 3):
                    for src, dst, n in parts(lax.rem(me.y + d, 4), i):
                        remote(src, dst, send.at[d, n], recv.at[i // 2, n], me.along_y(d)).start()
                for src, dst, n in parts(me.y, i):
                    pltpu.make_async_copy(src, dst, recv.at[i // 2, n]).start()

    spread(first_parts, ya_s, ya_r, range(SITES))
    spread(second_parts, yb_s, yb_r, range(SITES))

    row_group = lax.broadcasted_iota(jnp.int32, (B, B), 0) // 8
    env_copies[0].wait()

    def init(pair, _):
        both = rows_buf[pair].astype(F32)
        for part in range(2):
            tiled = jnp.concatenate([both[8 * part : 8 * part + 8]] * (B // 8), axis=0)
            x_bufs[0][2 * pair + part, 2] = jnp.where(row_group == me.op, tiled, 0.0).astype(BF16)
        return 0

    lax.fori_loop(0, SECTORS // 2, init, 0)


    beside = me.along_x(1 + 2 * me.l)
    across = me.along_x(3 - 2 * me.l)
    last = SITES - 1

    def wanted(i):
        return own(i) if i == last else me.h >= 0

    def send_second(i):
        part = a_bufs[i].at[me.l, :, me.c, second]
        for n, device in enumerate([beside] if i == last else [across, beside, me.along_x(2)]):
            remote(part, part, xb_s.at[i, n], xb_r.at[i, me.l], device).start()

    def p1(i):
        a = a_bufs[i]

        @pl.when(own(i))
        def _():
            part = a.at[me.l, me.z, me.c, first]
            arrival(part, ya_r.at[i // 2, 0])
            targets = [beside] if i == last else [across, beside, me.along_x(2)]
            for n, device in enumerate(targets):
                remote(part, part, xa_s.at[i, n], xa_r.at[i, me.l], device).start()
            if i < EARLY:
                part = a.at[me.l, me.z, me.c, second]
                arrival(part, yb_r.at[i // 2, 0])
                for d in (1, 3, 2):
                    remote(part, part, za_s.at[i, d - 1], za_r.at[i, me.z], me.along_z(d)).start()

    def p2(i):
        a = a_bufs[i]

        @pl.when(own(i))
        def _():
            if i < EARLY:
                for d in (1, 3, 2):
                    z = lax.rem(me.z + d, 4)
                    arrival(a.at[me.l, z, me.c, second], za_r.at[i, z])
            else:
                for n in range(2):
                    arrival(a.at[me.l, :, me.c, 2 + n], yb_r.at[i // 2, n])
            send_second(i)

        @pl.when(wanted(i))
        def _():
            for l in range(2):
                @pl.when(jnp.logical_not(jnp.logical_and(own(i), me.l == l)))
                def _():
                    arrival(a.at[l, me.z, me.c, first], xa_r.at[i, l])
            for d in (1, 3, 2):
                part = a.at[:, me.z, me.c, first]
                remote(part, part, zb_s.at[i, d - 1], zb_r.at[i, me.z], me.along_z(d)).start()

    def p3(i):
        a = a_bufs[i]

        @pl.when(wanted(i))
        def _():
            for d in (1, 3, 2):
                z = lax.rem(me.z + d, 4)
                arrival(a.at[:, z, me.c, first], zb_r.at[i, z])

            @pl.when(own(i))
            def _():
                arrival(a.at[1 - me.l, :, me.c, second], xb_r.at[i, 1 - me.l])

            @pl.when(jnp.logical_not(own(i)))
            def _():
                for l in range(2):
                    arrival(a.at[l, :, me.c, second], xb_r.at[i, l])
            part = a.at[:, :, me.c]
            remote(part, part, c_s.at[i], c_r.at[i], me.sibling()).start()

    def p4(i):
        @pl.when(wanted(i))
        def _():
            arrival(a_bufs[i].at[:, :, 1 - me.c], c_r.at[i])

    column = lax.broadcasted_iota(jnp.int32, (1, B), 1)
    row = lax.broadcasted_iota(jnp.int32, (B, 1), 0)

    def multiply_first(i):
        a, x = a_bufs[i], x_bufs[i]

        def first_product(e, _):
            wide, scale = [], []
            for s in range(STATES):
                r = ints[i, 8 + e, s]
                wide.append(a[r // 8, lax.rem(r // 2, 4), lax.rem(r, 2), s])
                live = column < ints[i, 4, r]
                scale.append(
                    [jnp.where(live, floats[i, k, s], 0.0) for k in range(2)]
                    + [jnp.where(live, 1.0, 0.0)]
                )
            product = jnp.dot(
                x[e].reshape(CHAINS * B, B), jnp.concatenate(wide, axis=1), preferred_element_type=F32
            )
            for s in range(STATES):
                s_buf[e, s] = jnp.concatenate(
                    [
                        (product[k * B : (k + 1) * B, s * B : (s + 1) * B] * scale[s][k]).astype(BF16)
                        for k in range(CHAINS)
                    ],
                    axis=1,
                )
            return 0

        lax.fori_loop(0, SECTORS, first_product, 0, unroll=UNROLL)

    def multiply_second(i):
        a, new, h = a_bufs[i], x_bufs[i + 1], h_bufs[i]

        def second_product(pair, _):
            blocks = []
            for part in range(2):
                r = 2 * pair + part
                scaled = jnp.concatenate([s_buf[ints[i, s, r], s] for s in range(STATES)], axis=0)
                tensor = a[pair // 4, lax.rem(pair, 4), part].reshape(STATES * B, B)
                mixed = lax.dot_general(
                    tensor, scaled, (((0,), (0,)), ((), ())), preferred_element_type=F32
                )
                mixed = jnp.where(row < ints[i, 4, r], mixed, 0.0)
                chains = [mixed[:, k * B : (k + 1) * B] for k in range(CHAINS)]
                chains[2] = chains[2] + floats[i, 2, 0] * chains[0] + floats[i, 2, 1] * chains[1]
                for k in range(CHAINS):
                    new[r, k] = chains[k].astype(BF16)
                blocks.append(chains[2].reshape(SECTORS, 8, B))
            h[:, :, pair] = jnp.concatenate(blocks, axis=1).astype(BF16).reshape(8, 2, 16, B)
            return 0

        lax.fori_loop(0, SECTORS // 2, second_product, 0, unroll=UNROLL // 2)

    quarter = [pl.ds(4 * j, 4) for j in range(4)]
    through = {2: (0, 3), 3: (1, 2)}

    def out(i):
        target = i // 2

        @pl.when(own(i))
        def _():
            for k in range(2):
                src, dst = x_bufs[i + 1].at[:, k], out_terms.at[me.y, k]
                direct = me.y != target
                if target in through and k == 1:
                    far, between = through[target]
                    direct = jnp.logical_and(direct, me.y != far)

                    @pl.when(me.y == far)
                    def _():
                        for j in range(4):
                            remote(
                                x_bufs[i + 1].at[quarter[j], k], relay_buf.at[quarter[j]],
                                relay_s.at[0, j], relay_r.at[0, j], me.row(between),
                            ).start()

                @pl.when(me.y == target)
                def _():
                    pltpu.make_async_copy(src, dst, out_r.at[me.y, k]).start()

                @pl.when(direct)
                def _():
                    remote(src, dst, out_s.at[target, k], out_r.at[me.y, k], me.row(target)).start()

    def pass_out(target):
        far, between = through[target]

        @pl.when(me.y == between)
        def _():
            for j in range(4):
                part = relay_buf.at[quarter[j]]
                arrival(part, relay_r.at[0, j])
                remote(
                    part, out_terms.at[far, 1, quarter[j]], relay_s.at[1, j], relay_r.at[1, j], me.row(target)
                ).start()

    def h1(i):
        @pl.when(own(i))
        def _():
            remote(h_bufs[i].at[:, 1 - me.c], core_buf.at[i // 2], h1_s.at[i // 2], h1_r.at[i // 2], me.sibling()).start()

    def h2(i):
        n = i // 2

        @pl.when(own(i))
        def _():
            arrival(core_buf.at[n], h1_r.at[n])
            for g in range(8):
                part_buf[n, g] = (
                    h_bufs[i][g, me.c].astype(F32) + core_buf[n, g].astype(F32)
                ).astype(BF16)
            for g in range(8):
                @pl.when(g_me != g)
                def _():
                    remote(part_buf.at[n, g], ring_buf.at[n, g_me], h2_s.at[n, g], h2_r.at[n, g_me], me.group(g)).start()

    def h3(i):
        n = i // 2

        @pl.when(own(i))
        def _():
            total = part_buf[n, g_me].astype(F32)
            for d in range(1, 8):
                g = lax.rem(g_me + d, 8)
                arrival(ring_buf.at[n, g], h2_r.at[n, g])
                total = total + ring_buf[n, g].astype(F32)
            final_buf[n] = total.astype(BF16)

            @pl.when(me.y == n)
            def _():
                pltpu.make_async_copy(final_buf.at[n], out_block.at[me.y], h3_r.at[me.y]).start()

            @pl.when(me.y != n)
            def _():
                remote(final_buf.at[n], out_block.at[me.y], h3_s.at[n], h3_r.at[me.y], me.row(n)).start()

    def ahead(stage, i):
        if i < SITES:
            stage(i)

    p1(0)
    for d in range(1, SITES):
        site = lax.rem(me.site + d, SITES)
        arrival(ints_all.at[site], param_r.at[0, site])
        arrival(floats_all.at[site], param_r.at[1, site])
    to_smem = [
        pltpu.make_async_copy(ints_all, ints, param_l.at[0]),
        pltpu.make_async_copy(floats_all, floats, param_l.at[1]),
    ]
    for copy in to_smem:
        copy.start()
    p1(1)
    p2(0)
    for copy in to_smem + env_copies[1:]:
        copy.wait()
    p1(2)
    p2(1)
    p3(0)
    for i in range(SITES):
        ahead(p2, i + 2)
        ahead(p1, i + 3)

        def before():
            p4(i)
            multiply_first(i)

        pl.when(wanted(i))(before)
        ahead(p3, i + 1)
        if i >= 1:
            h2(i - 1)
        pl.when(wanted(i))(lambda: multiply_second(i))
        out(i)
        h1(i)
        if i == SITES - 2:
            pass_out(2)
        if i >= 2:
            h3(i - 2)
    pass_out(3)
    h2(SITES - 1)
    h3(SITES - 2)
    h3(SITES - 1)

    for q in range(ROOTS):
        for k in range(2):
            relayed = [target for target in through if k == 1 and through[target][0] == q]
            for target in relayed:
                @pl.when(me.y != target)
                def _():
                    arrival(out_terms.at[q, k], out_r.at[q, k])

                @pl.when(me.y == target)
                def _():
                    for j in range(4):
                        arrival(out_terms.at[q, k, quarter[j]], relay_r.at[1, j])
            if not relayed:
                arrival(out_terms.at[q, k], out_r.at[q, k])
        arrival(out_block.at[q], h3_r.at[q])
    for copy in sends:
        copy.wait_send()

    def left(src, sem):
        pltpu.make_async_copy(src, src, sem).wait()

    for i in range(SITES):
        a = a_bufs[i]

        @pl.when(me.site == i)
        def _():
            for d in (1, 2, 3):
                for parts, sem in ((first_parts, ya_s), (second_parts, yb_s)):
                    for src, dst, n in parts(0, i):
                        left(dst, sem.at[d, n])

        @pl.when(own(i))
        def _():
            if i < EARLY:
                for d in (1, 2, 3):
                    left(a.at[0, 0, 0, first], za_s.at[i, d - 1])
            for n in range(1 if i == last else 3):
                left(a.at[0, 0, 0, first], xa_s.at[i, n])
            for n in range(1 if i == last else 3):
                left(a.at[0, :, 0, second], xb_s.at[i, n])
            left(core_buf.at[i // 2], h1_s.at[i // 2])
            for g in range(8):
                @pl.when(g_me != g)
                def _():
                    left(part_buf.at[i // 2, g], h2_s.at[i // 2, g])

            @pl.when(me.y != i // 2)
            def _():
                for k in range(2):
                    if i // 2 in through and k == 1:
                        @pl.when(me.y != through[i // 2][0])
                        def _():
                            left(x_bufs[i + 1].at[:, k], out_s.at[i // 2, k])
                    else:
                        left(x_bufs[i + 1].at[:, k], out_s.at[i // 2, k])
                left(final_buf.at[i // 2], h3_s.at[i // 2])

        @pl.when(wanted(i))
        def _():
            for d in (1, 2, 3):
                left(a.at[:, 0, 0, first], zb_s.at[i, d - 1])
            left(a.at[:, :, 0], c_s.at[i])
    for n, low in ((0, 0), (1, 2)):
        @pl.when(jnp.logical_or(me.y == low, me.y == low + 1))
        def _():
            for j in range(4):
                left(relay_buf.at[quarter[j]], relay_s.at[n, j])


def shards(mps, sector_map, live_rows, term_mask, term_coef, block_coef, env_terms, env_block):
    dma = pltpu.SemaphoreType.DMA
    vmem = pltpu.VMEM
    scratch = [vmem((2, 4, 2, STATES, B, B), BF16)] * SITES
    scratch += [vmem((SECTORS, CHAINS, B, B), BF16)] * (SITES + 1)
    scratch += [vmem((8, 2, 8, 16, B), BF16)] * SITES
    scratch += [
        vmem((SECTORS, STATES, B, CHAINS * B), BF16),
        vmem((4, 8, 8, 16, B), BF16),
        vmem((4, 8, 8, 16, B), BF16),
        vmem((4, 8, 8, 16, B), BF16),
        vmem((4, 8, 16, B), BF16),
        vmem((SITES, 24, B), jnp.int32),
        vmem((SITES, 8, B), F32),
        pltpu.SMEM((SITES, 24, B), jnp.int32),
        pltpu.SMEM((SITES, 8, B), F32),
        vmem((8, 16, B), BF16),
        vmem((SECTORS, B, B), BF16),
        dma((2, SITES)), dma((2, SITES)), dma((2,)),
        dma((4, 1)), dma((4, 1)), dma((4, 2)), dma((4, 2)),
        dma((SITES, 3)), dma((SITES, 2)),
        dma((SITES, 3)), dma((SITES, 4)),
        dma((SITES, 3)), dma((SITES, 2)),
        dma((SITES, 3)), dma((SITES, 4)),
        dma((SITES,)), dma((SITES,)),
        dma((3,)),
        dma((4, 2)), dma((4, 2)),
        dma((2, 4)), dma((2, 4)),
        dma((4,)), dma((4,)),
        dma((4, 8)), dma((4, 8)),
        dma((4,)), dma((4,)),
    ]
    anywhere = pl.BlockSpec(memory_space=pl.ANY)
    inside = pl.BlockSpec(memory_space=pltpu.VMEM)
    terms, block = pl.pallas_call(
        kernel,
        out_shape=(
            jax.ShapeDtypeStruct((ROOTS, 2, SECTORS, B, B), BF16),
            jax.ShapeDtypeStruct((ROOTS, 8, 16, B), BF16),
        ),
        in_specs=[inside] * 5 + [anywhere] * 3,
        out_specs=(anywhere, anywhere),
        scratch_shapes=scratch,
        compiler_params=pltpu.CompilerParams(
            collective_id=0, has_side_effects=True, vmem_limit_bytes=56 * 2**20
        ),
        name="chains",
    )(
        sector_map[0], live_rows, term_mask[0], term_coef[0], block_coef,
        env_block.reshape(ROOTS, 8, 16, B), mps[0].reshape(ROOTS, STATES, 2, 4, 2, B, B), env_terms,
    )
    return terms[None], block.reshape(1, ROOTS, SECTORS, 8, B)


def solution(mesh):
    in_specs = (
        P("site", None, None, None, None, None),
        P("site", None, None),
        P("site", None),
        P("site", "op", None),
        P("site", "op", None),
        P("site", "op"),
        P(None, "op", None, None, None),
        P(None, None, "op", None),
    )
    out_specs = (P("site", None, "op", None, None, None), P("site", None, None, "op", None))
    return jax.shard_map(shards, mesh=mesh, in_specs=in_specs, out_specs=out_specs, check_vma=False)
```

```python
import functools

import jax
import jax.numpy as jnp
from jax import lax
from jax.experimental import pallas as pl
from jax.experimental.pallas import tpu as pltpu
from jax.sharding import PartitionSpec as P

MESH = pl.DeviceIdType.MESH
F32 = jnp.float32
BF16 = jnp.bfloat16
SITES, ROOTS, STATES, SECTORS, B = 8, 4, 4, 16, 128
CHAINS = 3
UNROLL = 8
EARLY = 2


class Place:
    def __init__(self):
        site = lax.axis_index("site")
        op = lax.axis_index("op")
        self.site, self.op = site, op
        self.h, self.y = lax.rem(site, 2), site // 2
        self.l, self.z, self.c = op // 8, lax.rem(op // 2, 4), lax.rem(op, 2)
        self.x = 2 * self.h + self.l

    def along_x(self, by):
        x = lax.rem(self.x + by, 4)
        return {"site": 2 * self.y + x // 2, "op": 8 * lax.rem(x, 2) + 2 * self.z + self.c}

    def along_z(self, by):
        z = lax.rem(self.z + by, 4)
        return {"site": self.site, "op": 8 * self.l + 2 * z + self.c}

    def along_y(self, by):
        return {"site": 2 * lax.rem(self.y + by, 4) + self.h, "op": self.op}

    def row(self, y):
        return {"site": 2 * y + self.h, "op": self.op}

    def sibling(self):
        return {"site": self.site, "op": self.op + 1 - 2 * self.c}

    def along_site(self, by):
        return {"site": lax.rem(self.site + by, SITES), "op": self.op}

    def group(self, g):
        return {"site": self.site, "op": 2 * g + self.c}


def kernel(map_ref, live_ref, mask_ref, coef_ref, pair_ref, block_ref, mps_ref, env_ref, out_terms, out_block, *scratch):
    scratch = list(scratch)
    a_bufs = [scratch.pop(0) for _ in range(SITES)]
    x_bufs = [scratch.pop(0) for _ in range(SITES + 1)]
    h_bufs = [scratch.pop(0) for _ in range(SITES)]
    (s_buf, core_buf, part_buf, ring_buf, final_buf, ints_all, floats_all, ints, floats,
     rows_buf, relay_buf, param_s, param_r, param_l, ya_s, ya_r, yb_s, yb_r, xa_s, xa_r, za_s, za_r, xb_s, xb_r, zb_s, zb_r, c_s, c_r,
     env_l, out_s, out_r, relay_s, relay_r, h1_s, h1_r, h2_s, h2_r, h3_s, h3_r) = scratch
    me = Place()

    def remote(src, dst, send, recv, device):
        return pltpu.make_async_remote_copy(
            src_ref=src, dst_ref=dst, send_sem=send, recv_sem=recv, device_id=device, device_id_type=MESH
        )

    def arrival(dst, recv):
        pltpu.make_async_copy(dst, dst, recv).wait()

    env_copies = [pltpu.make_async_copy(block_ref.at[me.y], rows_buf, env_l.at[2])]
    for k in range(2):
        env_copies.append(pltpu.make_async_copy(env_ref.at[me.y, k], x_bufs[0].at[:, k], env_l.at[k]))
    for copy in env_copies:
        copy.start()

    source = lax.broadcasted_iota(jnp.int32, (SECTORS, SECTORS), 0)
    target = lax.broadcasted_iota(jnp.int32, (SECTORS, SECTORS), 1)
    lane = lax.broadcasted_iota(jnp.int32, (SECTORS, B), 1)
    inverse = jnp.zeros((SECTORS, B), jnp.int32)
    for s in range(STATES):
        found = jnp.max(jnp.where(map_ref[pl.ds(s, 1), :] == source, target, 0), axis=1, keepdims=True)
        inverse = jnp.where(lane == s, found, inverse)
    ints_all[me.site] = jnp.zeros((24, B), jnp.int32)
    ints_all[me.site, pl.ds(0, STATES), pl.ds(0, SECTORS)] = map_ref[...]
    ints_all[me.site, pl.ds(4, 1), pl.ds(0, SECTORS)] = live_ref[...]
    ints_all[me.site, pl.ds(8, SECTORS), :] = inverse
    floats_all[me.site] = jnp.zeros((8, B), F32)
    floats_all[me.site, pl.ds(0, 2), pl.ds(0, STATES)] = coef_ref[...] * mask_ref[...].astype(F32)
    floats_all[me.site, pl.ds(2, 1), pl.ds(0, 2)] = pair_ref[...]

    barrier = pltpu.get_barrier_semaphore()
    partners = [me.along_site(d) for d in range(1, SITES)]
    partners += [me.along_x(1), me.along_x(3)]
    partners += [me.along_z(d) for d in (1, 2, 3)]
    partners += [me.sibling()]
    g_me = me.op // 2
    partners += [
        {"site": me.site, "op": 8 * (1 - me.l) + 2 * lax.rem(me.z + d, 4) + me.c} for d in (1, 2, 3)
    ]
    for device in partners:
        pl.semaphore_signal(barrier, inc=1, device_id=device, device_id_type=MESH)
    pl.semaphore_wait(barrier, len(partners))

    sends = []

    def start(copy):
        copy.start()
        sends.append(copy)

    for d in range(1, SITES):
        start(remote(ints_all.at[me.site], ints_all.at[me.site], param_s.at[0, d], param_r.at[0, me.site], me.along_site(d)))
        start(remote(floats_all.at[me.site], floats_all.at[me.site], param_s.at[1, d], param_r.at[1, me.site], me.along_site(d)))

    first, second = pl.ds(0, 2), pl.ds(2, 2)

    def own(i):
        return me.h == i % 2

    def first_parts(q, i):
        return [(mps_ref.at[q, first, me.l, me.z, me.c], a_bufs[i].at[me.l, me.z, me.c, first], 0)]

    def second_parts(q, i):
        if i < EARLY:
            return [(mps_ref.at[q, second, me.l, me.z, me.c], a_bufs[i].at[me.l, me.z, me.c, second], 0)]
        return [(mps_ref.at[q, 2 + n, me.l, :, me.c], a_bufs[i].at[me.l, :, me.c, 2 + n], n) for n in range(2)]

    def spread(parts, send, recv, sites):
        for i in sites:
            @pl.when(me.site == i)
            def _():
                for d in (2, 1, 3):
                    for src, dst, n in parts(lax.rem(me.y + d, 4), i):
                        remote(src, dst, send.at[d, n], recv.at[i // 2, n], me.along_y(d)).start()
                for src, dst, n in parts(me.y, i):
                    pltpu.make_async_copy(src, dst, recv.at[i // 2, n]).start()

    spread(first_parts, ya_s, ya_r, range(SITES))
    spread(second_parts, yb_s, yb_r, range(SITES))

    row_group = lax.broadcasted_iota(jnp.int32, (B, B), 0) // 8
    env_copies[0].wait()

    def init(pair, _):
        both = rows_buf[pair].astype(F32)
        for part in range(2):
            tiled = jnp.concatenate([both[8 * part : 8 * part + 8]] * (B // 8), axis=0)
            x_bufs[0][2 * pair + part, 2] = jnp.where(row_group == me.op, tiled, 0.0).astype(BF16)
        return 0

    lax.fori_loop(0, SECTORS // 2, init, 0)


    beside = me.along_x(1 + 2 * me.l)
    across = me.along_x(3 - 2 * me.l)
    last = SITES - 1

    def wanted(i):
        return own(i) if i == last else me.h >= 0

    def send_second(i):
        part = a_bufs[i].at[me.l, :, me.c, second]
        for n, device in enumerate([beside] if i == last else [across, beside, me.along_x(2)]):
            remote(part, part, xb_s.at[i, n], xb_r.at[i, me.l], device).start()

    def p1(i):
        a = a_bufs[i]

        @pl.when(own(i))
        def _():
            part = a.at[me.l, me.z, me.c, first]
            arrival(part, ya_r.at[i // 2, 0])
            targets = [beside] if i == last else [across, beside, me.along_x(2)]
            for n, device in enumerate(targets):
                remote(part, part, xa_s.at[i, n], xa_r.at[i, me.l], device).start()
            if i < EARLY:
                part = a.at[me.l, me.z, me.c, second]
                arrival(part, yb_r.at[i // 2, 0])
                for d in (1, 3, 2):
                    remote(part, part, za_s.at[i, d - 1], za_r.at[i, me.z], me.along_z(d)).start()
            else:
                for n in range(2):
                    arrival(a.at[me.l, :, me.c, 2 + n], yb_r.at[i // 2, n])
                send_second(i)

    def p2(i):
        a = a_bufs[i]

        @pl.when(own(i))
        def _():
            if i < EARLY:
                for d in (1, 3, 2):
                    z = lax.rem(me.z + d, 4)
                    arrival(a.at[me.l, z, me.c, second], za_r.at[i, z])
                send_second(i)

        @pl.when(wanted(i))
        def _():
            for l in range(2):
                @pl.when(jnp.logical_not(jnp.logical_and(own(i), me.l == l)))
                def _():
                    arrival(a.at[l, me.z, me.c, first], xa_r.at[i, l])
            for d in (1, 3, 2):
                part = a.at[:, me.z, me.c, first]
                remote(part, part, zb_s.at[i, d - 1], zb_r.at[i, me.z], me.along_z(d)).start()

    def p3(i):
        a = a_bufs[i]

        @pl.when(wanted(i))
        def _():
            for d in (1, 3, 2):
                z = lax.rem(me.z + d, 4)
                arrival(a.at[:, z, me.c, first], zb_r.at[i, z])

            @pl.when(own(i))
            def _():
                arrival(a.at[1 - me.l, :, me.c, second], xb_r.at[i, 1 - me.l])

            @pl.when(jnp.logical_not(own(i)))
            def _():
                for l in range(2):
                    arrival(a.at[l, :, me.c, second], xb_r.at[i, l])
            part = a.at[:, :, me.c]
            remote(part, part, c_s.at[i], c_r.at[i], me.sibling()).start()

    def p4(i):
        @pl.when(wanted(i))
        def _():
            arrival(a_bufs[i].at[:, :, 1 - me.c], c_r.at[i])

    column = lax.broadcasted_iota(jnp.int32, (1, B), 1)
    row = lax.broadcasted_iota(jnp.int32, (B, 1), 0)

    def multiply_first(i):
        a, x = a_bufs[i], x_bufs[i]

        def first_product(e, _):
            wide, scale = [], []
            for s in range(STATES):
                r = ints[i, 8 + e, s]
                wide.append(a[r // 8, lax.rem(r // 2, 4), lax.rem(r, 2), s])
                live = column < ints[i, 4, r]
                scale.append(
                    [jnp.where(live, floats[i, k, s], 0.0) for k in range(2)]
                    + [jnp.where(live, 1.0, 0.0)]
                )
            product = jnp.dot(
                x[e].reshape(CHAINS * B, B), jnp.concatenate(wide, axis=1), preferred_element_type=F32
            )
            for s in range(STATES):
                s_buf[e, s] = jnp.concatenate(
                    [
                        (product[k * B : (k + 1) * B, s * B : (s + 1) * B] * scale[s][k]).astype(BF16)
                        for k in range(CHAINS)
                    ],
                    axis=1,
                )
            return 0

        lax.fori_loop(0, SECTORS, first_product, 0, unroll=UNROLL)

    def multiply_second(i):
        a, new, h = a_bufs[i], x_bufs[i + 1], h_bufs[i]

        def second_product(pair, _):
            blocks = []
            for part in range(2):
                r = 2 * pair + part
                scaled = jnp.concatenate([s_buf[ints[i, s, r], s] for s in range(STATES)], axis=0)
                tensor = a[pair // 4, lax.rem(pair, 4), part].reshape(STATES * B, B)
                mixed = lax.dot_general(
                    tensor, scaled, (((0,), (0,)), ((), ())), preferred_element_type=F32
                )
                mixed = jnp.where(row < ints[i, 4, r], mixed, 0.0)
                chains = [mixed[:, k * B : (k + 1) * B] for k in range(CHAINS)]
                chains[2] = chains[2] + floats[i, 2, 0] * chains[0] + floats[i, 2, 1] * chains[1]
                for k in range(CHAINS):
                    new[r, k] = chains[k].astype(BF16)
                blocks.append(chains[2].reshape(SECTORS, 8, B))
            h[:, :, pair] = jnp.concatenate(blocks, axis=1).astype(BF16).reshape(8, 2, 16, B)
            return 0

        lax.fori_loop(0, SECTORS // 2, second_product, 0, unroll=UNROLL // 2)

    quarter = [pl.ds(4 * j, 4) for j in range(4)]
    through = {2: (0, 3), 3: (1, 2)}

    def out(i):
        target = i // 2

        @pl.when(own(i))
        def _():
            for k in range(2):
                src, dst = x_bufs[i + 1].at[:, k], out_terms.at[me.y, k]
                direct = me.y != target
                if target in through and k == 1:
                    far, between = through[target]
                    direct = jnp.logical_and(direct, me.y != far)

                    @pl.when(me.y == far)
                    def _():
                        for j in range(4):
                            remote(
                                x_bufs[i + 1].at[quarter[j], k], relay_buf.at[quarter[j]],
                                relay_s.at[0, j], relay_r.at[0, j], me.row(between),
                            ).start()

                @pl.when(me.y == target)
                def _():
                    pltpu.make_async_copy(src, dst, out_r.at[me.y, k]).start()

                @pl.when(direct)
                def _():
                    remote(src, dst, out_s.at[target, k], out_r.at[me.y, k], me.row(target)).start()

    def pass_out(target):
        far, between = through[target]

        @pl.when(me.y == between)
        def _():
            for j in range(4):
                part = relay_buf.at[quarter[j]]
                arrival(part, relay_r.at[0, j])
                remote(
                    part, out_terms.at[far, 1, quarter[j]], relay_s.at[1, j], relay_r.at[1, j], me.row(target)
                ).start()

    def h1(i):
        @pl.when(own(i))
        def _():
            remote(h_bufs[i].at[:, 1 - me.c], core_buf.at[i // 2], h1_s.at[i // 2], h1_r.at[i // 2], me.sibling()).start()

    def h2(i):
        n = i // 2

        @pl.when(own(i))
        def _():
            arrival(core_buf.at[n], h1_r.at[n])
            for g in range(8):
                part_buf[n, g] = (
                    h_bufs[i][g, me.c].astype(F32) + core_buf[n, g].astype(F32)
                ).astype(BF16)
            for g in range(8):
                @pl.when(g_me != g)
                def _():
                    remote(part_buf.at[n, g], ring_buf.at[n, g_me], h2_s.at[n, g], h2_r.at[n, g_me], me.group(g)).start()

    def h3(i):
        n = i // 2

        @pl.when(own(i))
        def _():
            total = part_buf[n, g_me].astype(F32)
            for d in range(1, 8):
                g = lax.rem(g_me + d, 8)
                arrival(ring_buf.at[n, g], h2_r.at[n, g])
                total = total + ring_buf[n, g].astype(F32)
            final_buf[n] = total.astype(BF16)

            @pl.when(me.y == n)
            def _():
                pltpu.make_async_copy(final_buf.at[n], out_block.at[me.y], h3_r.at[me.y]).start()

            @pl.when(me.y != n)
            def _():
                remote(final_buf.at[n], out_block.at[me.y], h3_s.at[n], h3_r.at[me.y], me.row(n)).start()

    def ahead(stage, i):
        if i < SITES:
            stage(i)

    p1(0)
    for d in range(1, SITES):
        site = lax.rem(me.site + d, SITES)
        arrival(ints_all.at[site], param_r.at[0, site])
        arrival(floats_all.at[site], param_r.at[1, site])
    to_smem = [
        pltpu.make_async_copy(ints_all, ints, param_l.at[0]),
        pltpu.make_async_copy(floats_all, floats, param_l.at[1]),
    ]
    for copy in to_smem:
        copy.start()
    p1(1)
    p2(0)
    for copy in to_smem + env_copies[1:]:
        copy.wait()
    p1(2)
    p2(1)
    p3(0)
    for i in range(SITES):
        ahead(p2, i + 2)
        ahead(p1, i + 3)

        def before():
            p4(i)
            multiply_first(i)

        pl.when(wanted(i))(before)
        ahead(p3, i + 1)
        if i >= 1:
            h2(i - 1)
        pl.when(wanted(i))(lambda: multiply_second(i))
        out(i)
        h1(i)
        if i == SITES - 2:
            pass_out(2)
        if i >= 2:
            h3(i - 2)
    pass_out(3)
    h2(SITES - 1)
    h3(SITES - 2)
    h3(SITES - 1)

    for q in range(ROOTS):
        for k in range(2):
            relayed = [target for target in through if k == 1 and through[target][0] == q]
            for target in relayed:
                @pl.when(me.y != target)
                def _():
                    arrival(out_terms.at[q, k], out_r.at[q, k])

                @pl.when(me.y == target)
                def _():
                    for j in range(4):
                        arrival(out_terms.at[q, k, quarter[j]], relay_r.at[1, j])
            if not relayed:
                arrival(out_terms.at[q, k], out_r.at[q, k])
        arrival(out_block.at[q], h3_r.at[q])
    for copy in sends:
        copy.wait_send()

    def left(src, sem):
        pltpu.make_async_copy(src, src, sem).wait()

    for i in range(SITES):
        a = a_bufs[i]

        @pl.when(me.site == i)
        def _():
            for d in (1, 2, 3):
                for parts, sem in ((first_parts, ya_s), (second_parts, yb_s)):
                    for src, dst, n in parts(0, i):
                        left(dst, sem.at[d, n])

        @pl.when(own(i))
        def _():
            if i < EARLY:
                for d in (1, 2, 3):
                    left(a.at[0, 0, 0, first], za_s.at[i, d - 1])
            for n in range(1 if i == last else 3):
                left(a.at[0, 0, 0, first], xa_s.at[i, n])
            for n in range(1 if i == last else 3):
                left(a.at[0, :, 0, second], xb_s.at[i, n])
            left(core_buf.at[i // 2], h1_s.at[i // 2])
            for g in range(8):
                @pl.when(g_me != g)
                def _():
                    left(part_buf.at[i // 2, g], h2_s.at[i // 2, g])

            @pl.when(me.y != i // 2)
            def _():
                for k in range(2):
                    if i // 2 in through and k == 1:
                        @pl.when(me.y != through[i // 2][0])
                        def _():
                            left(x_bufs[i + 1].at[:, k], out_s.at[i // 2, k])
                    else:
                        left(x_bufs[i + 1].at[:, k], out_s.at[i // 2, k])
                left(final_buf.at[i // 2], h3_s.at[i // 2])

        @pl.when(wanted(i))
        def _():
            for d in (1, 2, 3):
                left(a.at[:, 0, 0, first], zb_s.at[i, d - 1])
            left(a.at[:, :, 0], c_s.at[i])
    for n, low in ((0, 0), (1, 2)):
        @pl.when(jnp.logical_or(me.y == low, me.y == low + 1))
        def _():
            for j in range(4):
                left(relay_buf.at[quarter[j]], relay_s.at[n, j])


def shards(mps, sector_map, live_rows, term_mask, term_coef, block_coef, env_terms, env_block):
    dma = pltpu.SemaphoreType.DMA
    vmem = pltpu.VMEM
    scratch = [vmem((2, 4, 2, STATES, B, B), BF16)] * SITES
    scratch += [vmem((SECTORS, CHAINS, B, B), BF16)] * (SITES + 1)
    scratch += [vmem((8, 2, 8, 16, B), BF16)] * SITES
    scratch += [
        vmem((SECTORS, STATES, B, CHAINS * B), BF16),
        vmem((4, 8, 8, 16, B), BF16),
        vmem((4, 8, 8, 16, B), BF16),
        vmem((4, 8, 8, 16, B), BF16),
        vmem((4, 8, 16, B), BF16),
        vmem((SITES, 24, B), jnp.int32),
        vmem((SITES, 8, B), F32),
        pltpu.SMEM((SITES, 24, B), jnp.int32),
        pltpu.SMEM((SITES, 8, B), F32),
        vmem((8, 16, B), BF16),
        vmem((SECTORS, B, B), BF16),
        dma((2, SITES)), dma((2, SITES)), dma((2,)),
        dma((4, 1)), dma((4, 1)), dma((4, 2)), dma((4, 2)),
        dma((SITES, 3)), dma((SITES, 2)),
        dma((SITES, 3)), dma((SITES, 4)),
        dma((SITES, 3)), dma((SITES, 2)),
        dma((SITES, 3)), dma((SITES, 4)),
        dma((SITES,)), dma((SITES,)),
        dma((3,)),
        dma((4, 2)), dma((4, 2)),
        dma((2, 4)), dma((2, 4)),
        dma((4,)), dma((4,)),
        dma((4, 8)), dma((4, 8)),
        dma((4,)), dma((4,)),
    ]
    anywhere = pl.BlockSpec(memory_space=pl.ANY)
    inside = pl.BlockSpec(memory_space=pltpu.VMEM)
    terms, block = pl.pallas_call(
        kernel,
        out_shape=(
            jax.ShapeDtypeStruct((ROOTS, 2, SECTORS, B, B), BF16),
            jax.ShapeDtypeStruct((ROOTS, 8, 16, B), BF16),
        ),
        in_specs=[inside] * 5 + [anywhere] * 3,
        out_specs=(anywhere, anywhere),
        scratch_shapes=scratch,
        compiler_params=pltpu.CompilerParams(
            collective_id=0, has_side_effects=True, vmem_limit_bytes=46 * 2**20
        ),
        name="chains",
    )(
        sector_map[0], live_rows, term_mask[0], term_coef[0], block_coef,
        env_block.reshape(ROOTS, 8, 16, B), mps[0].reshape(ROOTS, STATES, 2, 4, 2, B, B), env_terms,
    )
    return terms[None], block.reshape(1, ROOTS, SECTORS, 8, B)


def solution(mesh):
    in_specs = (
        P("site", None, None, None, None, None),
        P("site", None, None),
        P("site", None),
        P("site", "op", None),
        P("site", "op", None),
        P("site", "op"),
        P(None, "op", None, None, None),
        P(None, None, "op", None),
    )
    out_specs = (P("site", None, "op", None, None, None), P("site", None, None, "op", None))
    return jax.shard_map(shards, mesh=mesh, in_specs=in_specs, out_specs=out_specs, check_vma=False)
```
